256 devices in a mesh: outer: 16 (over x, y), inner: 16 (over z, core).
Axes of the slice: x: 4, y: 4, z: 8, core: 2. Of those that a mesh axis runs over, the one named last changes fastest.
Arguments:
- queries: bfloat16 [65536, 2048], P(('outer', 'inner')), may hold values from -16 to 16
- keys: bfloat16 [65536, 2048], P(('outer', 'inner')), may hold values from -4 to 4
- values: bfloat16 [65536, 2048], P(('outer', 'inner')), may hold values from -24 to 24
Outputs:
- attended: bfloat16 [65536, 2048], P(('outer', 'inner'))
The draws below stay inside these ranges and needn't reach their ends.
All inputs are finite; a program needn't handle non-finite values.
Results may differ from the reference program's by a relative error of at most 0.023.
Values may be sent and summed in bfloat16 or wider, within the bound.
No kernel may reach another device: no remote copies, remote signals or barrier semaphores. Data moves between devices by JAX's collectives and lax.ppermute only.
A program may use at most 128 MiB of HBM per device.

```python
import math
import jax
import jax.numpy as jnp
from jax import lax

HEADS = 16
HD = 128
LEVELS = 4
TOK_DEV = 256
WIDTH = 2048
SEQ = 65536
N_OUTER = 16
N_INNER = 16


def interpolate(anchors):
    row_ids = jnp.arange(SEQ, dtype=jnp.int32)
    lower_row = row_ids // 64
    fraction = ((row_ids % 64).astype(jnp.float32) / 64.0)[:, None]
    return anchors[lower_row] * (1.0 - fraction) + anchors[lower_row + 1] * fraction


def draw_keys(key, part):
    key = jax.random.fold_in(key, 11)
    key_anchor, key_rough = jax.random.split(key)
    anchors = 1.6 * jax.random.normal(key_anchor, (SEQ // 64 + 2, WIDTH), jnp.float32)
    rough_part = 0.9 * jax.random.normal(key_rough, (SEQ, WIDTH), jnp.float32)
    return jnp.clip(interpolate(anchors) + rough_part, -4.0, 4.0).astype(jnp.bfloat16)


def draw_queries(key, part):
    key = jax.random.fold_in(key, 23)
    key_anchor, key_rough = jax.random.split(key)
    anchors = 1.8 * jax.random.normal(key_anchor, (SEQ // 64 + 2, WIDTH), jnp.float32)
    rough_part = jax.random.normal(key_rough, (SEQ, WIDTH), jnp.float32)
    return jnp.clip(interpolate(anchors) + rough_part, -8.0, 8.0).astype(jnp.bfloat16)


def block_scale(stream_key, extent, shards, least, largest):
    gain = 1.0
    for axis_at, blocks in shards:
        steps = jax.random.uniform(jax.random.fold_in(jax.random.fold_in(stream_key, 6), axis_at), (blocks,), jnp.float32, least / len(shards), largest / len(shards))
        gain = gain * jnp.repeat(jnp.exp(steps), extent[axis_at] // blocks).reshape((-1,) + (1,) * (len(extent) - 1 - axis_at))
    return gain


def normal_values(rng, shape, width, limit, pieces=(), kind=jnp.bfloat16):
    values = width * jax.random.normal(rng, shape, jnp.float32)
    if pieces:
        values = values * block_scale(rng, shape, pieces, -0.22, 0.18)
    return jnp.clip(values, -limit, limit).astype(kind)


def setup_inputs(seed: int = 0) -> dict:
    seeds = jax.random.split(jax.random.key(seed), 4)
    return {
        "queries": draw_queries(jax.random.fold_in(seeds[3], 71), 0),
        "keys": draw_keys(jax.random.fold_in(seeds[3], 71), 0),
        "values": normal_values(seeds[2], (SEQ, WIDTH), 4.0, 24.0, ((0, 256),)),
    }


def halve_rows(block_rows):
    grouped = block_rows.astype(jnp.float32).reshape((block_rows.shape[0] // 2, 2) + block_rows.shape[1:])
    return lax.optimization_barrier(jnp.mean(grouped, axis=1)).astype(jnp.bfloat16)

def window_mean(block_rows, factor):
    grouped = block_rows.astype(jnp.float32).reshape((block_rows.shape[0] // factor, factor) + block_rows.shape[1:])
    return lax.optimization_barrier(jnp.mean(grouped, axis=1)).astype(jnp.bfloat16)

def split_view(matrix):
    return matrix.astype(jnp.float32).reshape(matrix.shape[0], HEADS, HD)

def far_level(coarse_query, far_key, far_value):
    score_scale = 1.0 / math.sqrt(HD)
    far_scores = jnp.einsum('qhd,khd->qhk', split_view(coarse_query), split_view(far_key)) * score_scale
    far_max = lax.optimization_barrier(jnp.max(far_scores, axis=2))
    far_weights = lax.optimization_barrier(jnp.exp(far_scores - far_max[:, :, None]).astype(jnp.bfloat16)).astype(jnp.float32)
    far_sum = lax.optimization_barrier(jnp.sum(far_weights, axis=2))
    far_numerator = jnp.einsum('qhk,khd->qhd', far_weights, split_view(far_value))
    return (far_max, far_sum, far_numerator)

def attend_block(own_query, near_keys, near_values, key_valid, far_parts):
    score_scale = 1.0 / math.sqrt(HD)
    near_scores = jnp.einsum('qhd,khd->qhk', split_view(own_query), split_view(near_keys)) * score_scale
    near_scores = jnp.where(key_valid[None, None, :], near_scores, -jnp.inf)
    row_max = lax.optimization_barrier(jnp.max(near_scores, axis=2))
    for factor, far_max, far_sum, far_numerator in far_parts:
        row_max = jnp.maximum(row_max, jnp.repeat(far_max, factor, axis=0))
    near_weights = lax.optimization_barrier(jnp.exp(near_scores - row_max[:, :, None]).astype(jnp.bfloat16)).astype(jnp.float32)
    weight_sum = lax.optimization_barrier(jnp.sum(near_weights, axis=2))
    numerator = jnp.einsum('qhk,khd->qhd', near_weights, split_view(near_values))
    for factor, far_max, far_sum, far_numerator in far_parts:
        level_scale = float(factor) * jnp.exp(jnp.repeat(far_max, factor, axis=0) - row_max)
        weight_sum = weight_sum + level_scale * jnp.repeat(far_sum, factor, axis=0)
        numerator = numerator + level_scale[:, :, None] * jnp.repeat(far_numerator, factor, axis=0)
    attended = numerator / weight_sum[:, :, None]
    return attended.reshape(own_query.shape[0], HEADS * HD).astype(jnp.bfloat16)

def reference(queries, keys, values):
    devices = N_OUTER * N_INNER
    seq_rows = TOK_DEV * devices
    half_rows = TOK_DEV // 2
    zeros_rows = jnp.zeros((TOK_DEV, queries.shape[1]), jnp.bfloat16)
    padded_keys = jnp.concatenate([zeros_rows, keys, zeros_rows], 0)
    padded_values = jnp.concatenate([zeros_rows, values, zeros_rows], 0)
    key_levels = [halve_rows(keys)]
    value_levels = [halve_rows(values)]
    coarse_levels = []
    for level_idx in range(1, LEVELS + 1):
        key_levels.append(halve_rows(key_levels[-1]))
        value_levels.append(halve_rows(value_levels[-1]))
        coarse_levels.append(window_mean(queries, 2 ** (level_idx + 1)))

    def device_rows(device_index):
        row_start = device_index * TOK_DEV
        own_query = lax.dynamic_slice_in_dim(queries, row_start, TOK_DEV, 0)
        near_keys = lax.dynamic_slice_in_dim(padded_keys, row_start, 3 * TOK_DEV, 0)
        near_values = lax.dynamic_slice_in_dim(padded_values, row_start, 3 * TOK_DEV, 0)
        position = row_start - TOK_DEV + jnp.arange(3 * TOK_DEV, dtype=jnp.int32)
        key_valid = (position >= 0) & (position < seq_rows)
        far_parts = []
        for level_idx in range(1, LEVELS + 1):
            factor = 2 ** (level_idx + 1)
            coarse_rows = TOK_DEV // factor
            coarse_query = lax.dynamic_slice_in_dim(coarse_levels[level_idx - 1], (device_index * coarse_rows).astype(jnp.int32), coarse_rows, 0)
            sibling_group = jnp.bitwise_xor(device_index // 2 ** level_idx, 1).astype(jnp.int32)
            far_key = lax.dynamic_slice_in_dim(key_levels[level_idx], (sibling_group * half_rows).astype(jnp.int32), half_rows, 0)
            far_value = lax.dynamic_slice_in_dim(value_levels[level_idx], (sibling_group * half_rows).astype(jnp.int32), half_rows, 0)
            far_parts.append((factor,) + far_level(coarse_query, far_key, far_value))
        return attend_block(own_query, near_keys, near_values, key_valid, far_parts)
    results = lax.map(device_rows, jnp.arange(devices, dtype=jnp.int32))
    return results.reshape(seq_rows, queries.shape[1])
```

```python
import math

import jax
import jax.numpy as jnp
from jax import lax
from jax.experimental import pallas as pl
from jax.experimental.pallas import tpu as pltpu
from jax.sharding import PartitionSpec as P

HEADS = 16
HD = 128
AXES = ("outer", "inner")
SCALE = math.log2(math.e) / math.sqrt(HD)
STEP_HEADS = 4
STEP_COLS = STEP_HEADS * HD
VMEM_LIMIT = 24 * 1024 * 1024


def averaging(rows, cols, row_span, col_span, weight):
    row = lax.broadcasted_iota(jnp.int32, (rows, cols), 0) // row_span
    col = lax.broadcasted_iota(jnp.int32, (rows, cols), 1) // col_span
    return jnp.where(row == col, weight, 0.0).astype(jnp.bfloat16)


def dot_f32(a, b):
    return lax.dot_general(a, b, (((1,), (0,)), ((), ())), preferred_element_type=jnp.float32)


def dot_nt(a, b):
    return lax.dot_general(a, b, (((1,), (1,)), ((), ())), preferred_element_type=jnp.float32)


def dot_bf16(a, b):
    return dot_f32(a, b).astype(jnp.bfloat16)


def summary_kernel(q_ref, k_ref, v_ref, first_ref, heads_ref, last_ref):
    rows = q_ref.shape[0]
    halves = [averaging(rows >> (i + 1), rows >> i, 1, 2, 0.5) for i in range(4)]
    levels = []
    for index, ref in enumerate((k_ref, v_ref)):
        current = ref[...]
        for matrix in halves[:2]:
            current = dot_bf16(matrix, current)
        first_ref[index] = current
        second = dot_bf16(halves[2], current)
        third = dot_bf16(halves[3], second)
        levels.append((second, third))
    coarse = dot_bf16(averaging(rows // 8, rows, 1, 8, 0.125), q_ref[...])
    n3 = rows // 16
    row = lax.broadcasted_iota(jnp.int32, (n3, n3), 0)
    col = lax.broadcasted_iota(jnp.int32, (n3, n3), 1) // 2
    place_k = jnp.where(row == col, 0.5, 0.0).astype(jnp.bfloat16)
    place_v = jnp.where(row == col + n3 // 2, 0.5, 0.0).astype(jnp.bfloat16)
    last = (dot_f32(place_k, levels[0][1]) + dot_f32(place_v, levels[1][1])).astype(jnp.bfloat16)
    n2 = rows // 8
    for h in range(STEP_HEADS):
        cols = slice(h * HD, (h + 1) * HD)
        heads_ref[h, 0:n2, :] = levels[0][0][:, cols]
        heads_ref[h, n2 : 2 * n2, :] = levels[1][0][:, cols]
        heads_ref[h, 2 * n2 : 3 * n2, :] = coarse[:, cols]
        last_ref[h] = last[:, cols]


def summaries(queries, keys, values):
    rows, width = queries.shape
    block = pl.BlockSpec((rows, STEP_COLS), lambda i: (0, i))
    return pl.pallas_call(
        summary_kernel,
        grid=(width // STEP_COLS,),
        in_specs=[block, block, block],
        out_specs=[
            pl.BlockSpec((2, rows // 4, STEP_COLS), lambda i: (0, 0, i)),
            pl.BlockSpec((STEP_HEADS, 3 * rows // 8, HD), lambda i: (i, 0, 0)),
            pl.BlockSpec((STEP_HEADS, rows // 16, HD), lambda i: (i, 0, 0)),
        ],
        out_shape=[
            jax.ShapeDtypeStruct((2, rows // 4, width), jnp.bfloat16),
            jax.ShapeDtypeStruct((HEADS, 3 * rows // 8, HD), jnp.bfloat16),
            jax.ShapeDtypeStruct((HEADS, rows // 16, HD), jnp.bfloat16),
        ],
        compiler_params=pltpu.CompilerParams(vmem_limit_bytes=VMEM_LIMIT),
        cost_estimate=pl.CostEstimate(flops=400_000_000, bytes_accessed=5_000_000, transcendentals=0),
        name="summaries",
    )(queries, keys, values)


def with_ones(value):
    return jnp.concatenate([value, jnp.ones_like(value)], 1)


def far_kernel(recv_ref, sib_ref, out_ref):
    blocks = recv_ref.shape[0]
    n2 = recv_ref.shape[1] // 3
    total = blocks * n2
    keys2 = recv_ref[:, 0:n2, :].reshape(total, HD)
    values2 = recv_ref[:, n2 : 2 * n2, :].reshape(total, HD)
    query2 = recv_ref[:, 2 * n2 : 3 * n2, :].reshape(total, HD)
    last = sib_ref[...].reshape(-1, HD)
    rows4 = last.shape[0] // 2
    row = lax.broadcasted_iota(jnp.int32, (rows4, 2 * rows4), 0)
    col = lax.broadcasted_iota(jnp.int32, (rows4, 2 * rows4), 1)
    span = sib_ref.shape[1] // 2
    spot = row + (row // span) * span
    keys4 = dot_bf16(jnp.where(col == spot, 1.0, 0.0).astype(jnp.bfloat16), last)
    values4 = dot_bf16(jnp.where(col == spot + span, 1.0, 0.0).astype(jnp.bfloat16), last)
    group = total // 4
    half = averaging(group // 2, group, 1, 2, 0.5)
    keys3 = [dot_bf16(half, keys2[i * group : (i + 1) * group]) for i in range(4)]
    values3 = [dot_bf16(half, values2[i * group : (i + 1) * group]) for i in range(4)]
    spread2 = averaging(group, group, 2, 2, 0.5)
    spread4 = averaging(group, group, 4, 4, 0.25)
    eye = (
        lax.broadcasted_iota(jnp.int32, (group, group), 0)
        == lax.broadcasted_iota(jnp.int32, (group, group), 1)
    )
    group_blocks = blocks // 4
    pad_row = lax.broadcasted_iota(jnp.int32, (16, group), 0)
    for g in range(4):
        own = query2[g * group : (g + 1) * group]
        sib = g ^ 1
        far = 2 * ((g // 2) ^ 1)
        key3 = jnp.concatenate(keys3[far : far + 2], 0)
        value3 = jnp.concatenate(values3[far : far + 2], 0)
        scores = [
            dot_nt(own, keys2[sib * group : (sib + 1) * group]) * SCALE + 3.0,
            dot_nt(dot_bf16(spread2, own), key3) * SCALE + 4.0,
            dot_nt(dot_bf16(spread4, own), keys4) * SCALE + 5.0,
        ]
        scores = jnp.concatenate(scores, 1)
        peak = jnp.max(scores, axis=1, keepdims=True)
        weights = jnp.exp2(scores - peak).astype(jnp.bfloat16)
        value = jnp.concatenate([values2[sib * group : (sib + 1) * group], value3, values4], 0)
        both = dot_f32(weights, with_ones(value))
        total_weight = both[:, HD:]
        mean = (both[:, :HD] / total_weight).astype(jnp.bfloat16)
        level = peak + jnp.log2(total_weight)
        level_row = jnp.sum(jnp.where(eye, level, 0.0), axis=0, keepdims=True)
        high = level_row.astype(jnp.bfloat16).astype(jnp.float32)
        rest = level_row - high
        mid = rest.astype(jnp.bfloat16).astype(jnp.float32)
        low = rest - mid
        packed = jnp.where(pad_row == 0, high, jnp.where(pad_row == 1, mid, low)).astype(jnp.bfloat16)
        for j in range(group_blocks):
            out_ref[g * group_blocks + j, 0:n2, :] = mean[j * n2 : (j + 1) * n2]
            out_ref[g * group_blocks + j, n2 : n2 + 16, :] = packed


def far_attention(received, sibling):
    blocks, packed_rows, _ = received.shape
    n2 = packed_rows // 3
    return pl.pallas_call(
        far_kernel,
        out_shape=jax.ShapeDtypeStruct((blocks, n2 + 16, HD), jnp.bfloat16),
        compiler_params=pltpu.CompilerParams(vmem_limit_bytes=VMEM_LIMIT),
        cost_estimate=pl.CostEstimate(
            flops=200_000_000, bytes_accessed=1_000_000, transcendentals=200_000
        ),
        name="far_attention",
    )(received, sibling)


def near_kernel(
    bias_ref, q_ref, k_ref, v_ref, kb_ref, vb_ref, ka_ref, va_ref, f1_ref, f2_ref, out_ref, level_ref
):
    rows = q_ref.shape[0]
    step = pl.program_id(0)
    coarse = dot_bf16(averaging(rows, rows, 4, 4, 0.25), q_ref[...])
    lane = lax.broadcasted_iota(jnp.int32, (rows, HD), 1)
    levels = jnp.zeros((rows, HD), jnp.float32)
    for h in range(STEP_HEADS):
        cols = slice(h * HD, (h + 1) * HD)
        query = q_ref[:, cols]
        far_key = jnp.concatenate([f1_ref[0, :, cols], f2_ref[0, :, cols]], 0)
        far_value = jnp.concatenate([f1_ref[1, :, cols], f2_ref[1, :, cols]], 0)
        scores = [
            dot_nt(query, k_ref[:, cols]) * SCALE,
            dot_nt(query, kb_ref[:, cols]) * SCALE + bias_ref[0],
            dot_nt(query, ka_ref[:, cols]) * SCALE + bias_ref[1],
            dot_nt(coarse[:, cols], far_key) * SCALE + 2.0,
        ]
        scores = jnp.concatenate(scores, 1)
        peak = jnp.max(scores, axis=1, keepdims=True)
        weights = jnp.exp2(scores - peak).astype(jnp.bfloat16)
        value = jnp.concatenate([v_ref[:, cols], vb_ref[:, cols], va_ref[:, cols], far_value], 0)
        both = dot_f32(weights, with_ones(value))
        total_weight = both[:, HD:]
        out_ref[:, cols] = (both[:, :HD] / total_weight).astype(jnp.bfloat16)
        level = peak + jnp.log2(total_weight)
        levels = jnp.where(lane == step * STEP_HEADS + h, level, levels)

    @pl.when(step == 0)
    def _():
        level_ref[...] = levels

    @pl.when(step > 0)
    def _():
        level_ref[...] = level_ref[...] + levels


def near_attention(bias, q, k, v, k_before, v_before, k_after, v_after, far1, far2):
    rows, width = q.shape
    block = pl.BlockSpec((rows, STEP_COLS), lambda i: (0, i))
    far_block = pl.BlockSpec((2, rows // 4, STEP_COLS), lambda i: (0, 0, i))
    return pl.pallas_call(
        near_kernel,
        grid=(width // STEP_COLS,),
        in_specs=[pl.BlockSpec(memory_space=pltpu.SMEM)] + [block] * 7 + [far_block] * 2,
        out_specs=[block, pl.BlockSpec((rows, HD), lambda i: (0, 0))],
        out_shape=[
            jax.ShapeDtypeStruct((rows, width), jnp.bfloat16),
            jax.ShapeDtypeStruct((rows, HD), jnp.float32),
        ],
        compiler_params=pltpu.CompilerParams(vmem_limit_bytes=VMEM_LIMIT),
        cost_estimate=pl.CostEstimate(
            flops=4_000_000_000, bytes_accessed=10_000_000, transcendentals=4_000_000
        ),
        name="near_attention",
    )(bias, q, k, v, k_before, v_before, k_after, v_after, far1, far2)


def combine_kernel(spot_ref, near_ref, level_ref, far_ref, out_ref):
    rows = near_ref.shape[0]
    n2 = far_ref.shape[1] - 16
    factor = rows // n2
    row = lax.broadcasted_iota(jnp.int32, (rows, HD), 0) // factor
    lane = lax.broadcasted_iota(jnp.int32, (rows, HD), 1)
    pick = jnp.where(lane == row + spot_ref[0], 1.0, 0.0).astype(jnp.bfloat16)
    spread = averaging(rows, n2, factor, 1, 1.0)
    parts = far_ref[:, n2 : n2 + 16, :]
    packed = parts.reshape(HEADS * 16, HD)
    spread_levels = dot_nt(pick, packed)
    heads = lax.broadcasted_iota(jnp.int32, (rows, HD), 1)
    for h in range(HEADS):
        cols = slice(h * HD, (h + 1) * HD)
        far_level = (
            spread_levels[:, 16 * h : 16 * h + 1]
            + spread_levels[:, 16 * h + 1 : 16 * h + 2]
            + spread_levels[:, 16 * h + 2 : 16 * h + 3]
        )
        near_part = 1.0 / (1.0 + jnp.exp2(far_level - level_ref[:, h : h + 1]))
        far_mean = dot_f32(spread, far_ref[h, 0:n2, :])
        near_mean = near_ref[:, cols].astype(jnp.float32)
        out_ref[:, cols] = (far_mean + near_part * (near_mean - far_mean)).astype(jnp.bfloat16)


def combine(spot, near_mean, near_level, far):
    return pl.pallas_call(
        combine_kernel,
        in_specs=[pl.BlockSpec(memory_space=pltpu.SMEM)]
        + [pl.BlockSpec(memory_space=pltpu.VMEM)] * 3,
        out_specs=pl.BlockSpec(memory_space=pltpu.VMEM),
        out_shape=jax.ShapeDtypeStruct(near_mean.shape, jnp.bfloat16),
        compiler_params=pltpu.CompilerParams(vmem_limit_bytes=VMEM_LIMIT),
        name="combine",
    )(spot, near_mean, near_level, far)


def body(queries, keys, values):
    devices = lax.axis_size(AXES)
    inner = lax.axis_size("inner")
    index = lax.axis_index(AXES)
    rows = queries.shape[0]
    n2 = rows // 8

    def exchange(value, stride):
        return lax.ppermute(value, AXES, [(i, i ^ stride) for i in range(devices)])

    first, heads, last = summaries(queries, keys, values)
    sibling = exchange(last, inner)
    up = [(i, i + 1) for i in range(devices - 1)]
    down = [(i + 1, i) for i in range(devices - 1)]
    packed = jnp.concatenate([heads, sibling], 1)
    received = lax.all_to_all(packed, "inner", 0, 0, tiled=True)
    far1 = exchange(first, 2)
    far2 = exchange(far1, 1)
    k_before = lax.ppermute(keys, AXES, up)
    k_after = lax.ppermute(keys, AXES, down)
    v_before = lax.ppermute(values, AXES, up)
    v_after = lax.ppermute(values, AXES, down)
    far = far_attention(received[:, : 3 * n2], received[:, 3 * n2 :])
    far = lax.all_to_all(far, "inner", 0, 0, tiled=True)
    lowest = jnp.float32(-1e30)
    bias = jnp.stack(
        [jnp.where(index == 0, lowest, 0.0), jnp.where(index == devices - 1, lowest, 0.0)]
    )
    near_mean, near_level = near_attention(
        bias, queries, keys, values, k_before, v_before, k_after, v_after, far1, far2
    )
    spot = (index % (inner // 4) * n2).reshape(1).astype(jnp.int32)
    return combine(spot, near_mean, near_level, far)


def solution(mesh):
    spec = P(AXES, None)
    return jax.shard_map(
        body, mesh=mesh, in_specs=(spec, spec, spec), out_specs=spec, check_vma=False
    )
```

```python
import functools
import math

import jax
import jax.numpy as jnp
from jax import lax
from jax.experimental import pallas as pl
from jax.experimental.pallas import tpu as pltpu
from jax.sharding import PartitionSpec as P

HEADS = 16
HD = 128
AXES = ("outer", "inner")
SCALE = math.log2(math.e) / math.sqrt(HD)
STEP_HEADS = 4
STEP_COLS = STEP_HEADS * HD
VMEM_LIMIT = 60 * 1024 * 1024


def grid_of(shape, axis, span=1):
    return lax.shift_right_logical(
        lax.broadcasted_iota(jnp.int32, shape, axis), jnp.int32(span.bit_length() - 1)
    )


def averaging(rows, cols, row_span, col_span, weight):
    same = grid_of((rows, cols), 0, row_span) == grid_of((rows, cols), 1, col_span)
    return jnp.where(same, weight, 0.0).astype(jnp.bfloat16)


def dot_f32(a, b):
    return lax.dot_general(a, b, (((1,), (0,)), ((), ())), preferred_element_type=jnp.float32)


def dot_nt(a, b):
    return lax.dot_general(a, b, (((1,), (1,)), ((), ())), preferred_element_type=jnp.float32)


def dot_bf16(a, b):
    return dot_f32(a, b).astype(jnp.bfloat16)


def summary_kernel(q_ref, k_ref, v_ref, first_ref, heads_ref, last_ref):
    rows = q_ref.shape[0]
    n1, n2, n4 = rows // 4, rows // 8, rows // 32
    nothing = jnp.zeros((n4, rows), jnp.bfloat16)
    top = [averaging(n1, rows, 1, 4, 1 / 4), averaging(n2, rows, 1, 8, 1 / 8)]
    bottom = averaging(n4, rows, 1, 32, 1 / 32)
    of_k = dot_f32(jnp.concatenate(top + [bottom, nothing], 0), k_ref[...])
    of_v = dot_f32(jnp.concatenate(top + [nothing, bottom], 0), v_ref[...])
    coarse = dot_bf16(top[1], q_ref[...])
    first_ref[0] = of_k[:n1].astype(jnp.bfloat16)
    first_ref[1] = of_v[:n1].astype(jnp.bfloat16)
    second_k = of_k[n1 : n1 + n2].astype(jnp.bfloat16)
    second_v = of_v[n1 : n1 + n2].astype(jnp.bfloat16)
    last = (of_k[n1 + n2 :] + of_v[n1 + n2 :]).astype(jnp.bfloat16)
    for h in range(STEP_HEADS):
        cols = slice(h * HD, (h + 1) * HD)
        heads_ref[h, 0:n2, :] = second_k[:, cols]
        heads_ref[h, n2 : 2 * n2, :] = second_v[:, cols]
        heads_ref[h, 2 * n2 : 3 * n2, :] = coarse[:, cols]
        last_ref[h] = last[:, cols]


def summaries(queries, keys, values):
    rows, width = queries.shape
    block = pl.BlockSpec((rows, STEP_COLS), lambda i: (0, i))
    return pl.pallas_call(
        summary_kernel,
        grid=(width // STEP_COLS,),
        in_specs=[block, block, block],
        out_specs=[
            pl.BlockSpec((2, rows // 4, STEP_COLS), lambda i: (0, 0, i)),
            pl.BlockSpec((STEP_HEADS, 7 * rows // 16, HD), lambda i: (i, 0, 0)),
            pl.BlockSpec((STEP_HEADS, rows // 16, HD), lambda i: (i, 0, 0)),
        ],
        out_shape=[
            jax.ShapeDtypeStruct((2, rows // 4, width), jnp.bfloat16),
            jax.ShapeDtypeStruct((HEADS, 7 * rows // 16, HD), jnp.bfloat16),
            jax.ShapeDtypeStruct((HEADS, rows // 16, HD), jnp.bfloat16),
        ],
        compiler_params=pltpu.CompilerParams(vmem_limit_bytes=VMEM_LIMIT),
        cost_estimate=pl.CostEstimate(flops=400_000_000, bytes_accessed=5_000_000, transcendentals=0),
        name="summaries",
    )(queries, keys, values)


def place_kernel(heads_ref, sibling_ref, out_ref):
    del heads_ref
    out_ref[...] = sibling_ref[...]


def place_sibling(heads, sibling):
    count, rows, _ = sibling.shape
    place = heads.shape[1] // rows - 1
    return pl.pallas_call(
        place_kernel,
        grid=(1,),
        in_specs=[
            pl.BlockSpec(memory_space=pl.ANY),
            pl.BlockSpec((count, rows, HD), lambda i: (0, 0, 0)),
        ],
        out_specs=pl.BlockSpec((count, rows, HD), lambda i: (0, place, 0)),
        out_shape=jax.ShapeDtypeStruct(heads.shape, heads.dtype),
        input_output_aliases={0: 0},
        compiler_params=pltpu.CompilerParams(vmem_limit_bytes=VMEM_LIMIT),
        name="place_sibling",
    )(heads, sibling)


def with_ones(value):
    return jnp.concatenate([value, jnp.ones_like(value)], 1)


def far_kernel(n2, recv_ref, level_ref, out_ref):
    del level_ref
    blocks = recv_ref.shape[0]
    total = blocks * n2
    keys2 = recv_ref[:, 0:n2, :].reshape(total, HD)
    values2 = recv_ref[:, n2 : 2 * n2, :].reshape(total, HD)
    query2 = recv_ref[:, 2 * n2 : 3 * n2, :].reshape(total, HD)
    last = recv_ref[:, 3 * n2 :, :].reshape(-1, HD)
    rows4 = last.shape[0] // 2
    row = lax.broadcasted_iota(jnp.int32, (rows4, 2 * rows4), 0)
    col = lax.broadcasted_iota(jnp.int32, (rows4, 2 * rows4), 1)
    span = n2 // 4
    spot = row + grid_of((rows4, 2 * rows4), 0, span) * span
    keys4 = dot_bf16(jnp.where(col == spot, 1.0, 0.0).astype(jnp.bfloat16), last)
    values4 = dot_bf16(jnp.where(col == spot + span, 1.0, 0.0).astype(jnp.bfloat16), last)
    group = total // 4
    half = averaging(group // 2, group, 1, 2, 0.5)
    keys3 = [dot_bf16(half, keys2[i * group : (i + 1) * group]) for i in range(4)]
    values3 = [dot_bf16(half, values2[i * group : (i + 1) * group]) for i in range(4)]
    spread2 = averaging(group, group, 2, 2, 0.5)
    spread4 = averaging(group, group, 4, 4, 0.25)
    eye = (
        lax.broadcasted_iota(jnp.int32, (group, group), 0)
        == lax.broadcasted_iota(jnp.int32, (group, group), 1)
    )
    group_blocks = blocks // 4
    pad_lane = grid_of((16, group), 1, n2)
    for g in range(4):
        own = query2[g * group : (g + 1) * group]
        sib = g ^ 1
        far = 2 * ((g // 2) ^ 1)
        key3 = jnp.concatenate(keys3[far : far + 2], 0)
        value3 = jnp.concatenate(values3[far : far + 2], 0)
        scores = [
            dot_nt(own, keys2[sib * group : (sib + 1) * group]) * SCALE + 3.0,
            dot_nt(dot_bf16(spread2, own), key3) * SCALE + 4.0,
            dot_nt(dot_bf16(spread4, own), keys4) * SCALE + 5.0,
        ]
        scores = jnp.concatenate(scores, 1)
        peak = jnp.max(scores, axis=1, keepdims=True)
        weights = jnp.exp2(scores - peak).astype(jnp.bfloat16)
        value = jnp.concatenate([values2[sib * group : (sib + 1) * group], value3, values4], 0)
        both = dot_f32(weights, with_ones(value))
        total_weight = both[:, HD:]
        mean = (both[:, :HD] * pl.reciprocal(total_weight, approx=True)).astype(jnp.bfloat16)
        level = peak + jnp.log2(total_weight)
        level_row = jnp.sum(jnp.where(eye, level, 0.0), axis=0, keepdims=True)
        level_rows = jnp.broadcast_to(level_row, (16, group))
        high = level_rows.astype(jnp.bfloat16).astype(jnp.float32)
        rest = level_rows - high
        mid = rest.astype(jnp.bfloat16).astype(jnp.float32)
        low = rest - mid
        for j in range(group_blocks):
            packed = jnp.zeros_like(high)
            for place, part in enumerate((high, mid, low)):
                turned = pltpu.roll(part, (place - j) * n2 % group, 1)
                packed = jnp.where(pad_lane == place, turned, packed)
            out_ref[g * group_blocks + j, 0:n2, :] = mean[j * n2 : (j + 1) * n2]
            out_ref[g * group_blocks + j, n2 : n2 + 16, :] = packed.astype(jnp.bfloat16)


def far_attention(received, n2, level):
    blocks = received.shape[0]
    vmem = pl.BlockSpec(memory_space=pltpu.VMEM)
    return pl.pallas_call(
        functools.partial(far_kernel, n2),
        in_specs=[vmem, pl.BlockSpec(memory_space=pl.ANY)],
        out_specs=vmem,
        out_shape=jax.ShapeDtypeStruct((blocks, n2 + 16, HD), jnp.bfloat16),
        compiler_params=pltpu.CompilerParams(vmem_limit_bytes=VMEM_LIMIT),
        cost_estimate=pl.CostEstimate(
            flops=200_000_000, bytes_accessed=1_000_000, transcendentals=200_000
        ),
        name="far_attention",
    )(received, level)


def softmax_parts(scores, offsets, top):
    chunks = [[s[:, i : i + HD] for i in range(0, s.shape[1], HD)] for s in scores]
    for parts, offset in zip(chunks, offsets):
        most = functools.reduce(jnp.maximum, parts) * SCALE + offset
        top = most if top is None else jnp.maximum(top, most)
    peak = jnp.broadcast_to(jnp.max(top, axis=1, keepdims=True), top.shape)
    weights = []
    for parts, offset in zip(chunks, offsets):
        shift = peak - offset
        weights += [jnp.exp2(s * SCALE - shift).astype(jnp.bfloat16) for s in parts]
    return weights, peak


def chip_kernel(q_ref, k_ref, v_ref, km_ref, vm_ref, f2_ref, mean_ref, level_ref):
    del f2_ref
    rows = q_ref.shape[0]
    step = pl.program_id(0)
    lane = lax.broadcasted_iota(jnp.int32, (rows, HD), 1)

    def scores_of(h):
        cols = slice(h * HD, (h + 1) * HD)
        return [dot_nt(q_ref[:, cols], ref[:, cols]) for ref in (k_ref, km_ref)]

    levels = jnp.zeros((rows, HD), jnp.float32)
    following = scores_of(0)
    for h in range(STEP_HEADS):
        current = following
        if h + 1 < STEP_HEADS:
            following = scores_of(h + 1)
        cols = slice(h * HD, (h + 1) * HD)
        weights, peak = softmax_parts(current, [0.0, 0.0], None)
        value = jnp.concatenate([v_ref[:, cols], vm_ref[:, cols]], 0)
        both = dot_f32(jnp.concatenate(weights, 1), with_ones(value))
        total = both[:, HD:]
        mean_ref[:, cols] = (both[:, :HD] * pl.reciprocal(total, approx=True)).astype(jnp.bfloat16)
        levels = jnp.where(lane == h, peak + jnp.log2(total), levels)
    level_ref[0] = levels


def chip_attention(q, k, v, k_mate, v_mate, far2):
    rows, width = q.shape
    steps = width // STEP_COLS
    block = pl.BlockSpec((rows, STEP_COLS), lambda i: (0, i))
    return pl.pallas_call(
        chip_kernel,
        grid=(steps,),
        in_specs=[block] * 5 + [pl.BlockSpec(memory_space=pl.ANY)],
        out_specs=[block, pl.BlockSpec((1, rows, HD), lambda i: (i, 0, 0))],
        out_shape=[
            jax.ShapeDtypeStruct((rows, width), jnp.bfloat16),
            jax.ShapeDtypeStruct((steps, rows, HD), jnp.float32),
        ],
        compiler_params=pltpu.CompilerParams(vmem_limit_bytes=VMEM_LIMIT),
        cost_estimate=pl.CostEstimate(
            flops=2_000_000_000, bytes_accessed=7_000_000, transcendentals=2_000_000
        ),
        name="chip_attention",
    )(q, k, v, k_mate, v_mate, far2)


def cross_kernel(
    bias_ref, q_ref, kc_ref, f1_ref, f2_ref, mean_ref, level_ref,
    weight_ref, sum_ref, peak_ref, total_ref,
):
    rows = q_ref.shape[0]
    coarse = dot_bf16(averaging(rows, rows, 4, 4, 0.25), q_ref[...])
    lane = lax.broadcasted_iota(jnp.int32, (rows, HD), 1)
    offsets = [bias_ref[0], 2.0]

    def scores_of(h):
        cols = slice(h * HD, (h + 1) * HD)
        far_key = jnp.concatenate([f1_ref[0, :, cols], f2_ref[0, :, cols]], 0)
        return [dot_nt(q_ref[:, cols], kc_ref[:, cols]), dot_nt(coarse[:, cols], far_key)]

    peaks = jnp.zeros((rows, HD), jnp.float32)
    totals = jnp.zeros((rows, HD), jnp.float32)
    following = scores_of(0)
    for h in range(STEP_HEADS):
        scores = following
        if h + 1 < STEP_HEADS:
            following = scores_of(h + 1)
        cols = slice(h * HD, (h + 1) * HD)
        chip = jnp.broadcast_to(level_ref[0, :, h : h + 1], (rows, HD))
        weights, peak = softmax_parts(scores, offsets, chip)
        weight_ref[h] = jnp.concatenate(weights[:-1], 1)
        value = jnp.concatenate([f1_ref[1, :, cols], f2_ref[1, :, cols]], 0)
        both = dot_f32(weights[-1], with_ones(value))
        chip_weight = jnp.exp2(chip - peak)
        sums = both[:, :HD] + chip_weight * mean_ref[:, cols].astype(jnp.float32)
        sum_ref[:, cols] = sums.astype(jnp.bfloat16)
        peaks = jnp.where(lane == h, peak, peaks)
        totals = jnp.where(lane == h, both[:, HD:] + chip_weight, totals)
    peak_ref[0] = peaks
    total_ref[0] = totals


def cross_attention(bias, q, k_cross, far1, far2, mean, level):
    rows, width = q.shape
    block = pl.BlockSpec((rows, STEP_COLS), lambda i: (0, i))
    far_block = pl.BlockSpec((2, rows // 4, STEP_COLS), lambda i: (0, 0, i))
    levels = pl.BlockSpec((1, rows, HD), lambda i: (i, 0, 0))
    return pl.pallas_call(
        cross_kernel,
        grid=(width // STEP_COLS,),
        in_specs=[pl.BlockSpec(memory_space=pltpu.SMEM)]
        + [block] * 2
        + [far_block] * 2
        + [block, levels],
        out_specs=[pl.BlockSpec((STEP_HEADS, rows, rows), lambda i: (i, 0, 0)), block, levels, levels],
        out_shape=[
            jax.ShapeDtypeStruct((HEADS, rows, rows), jnp.bfloat16),
            jax.ShapeDtypeStruct(mean.shape, mean.dtype),
            jax.ShapeDtypeStruct(level.shape, level.dtype),
            jax.ShapeDtypeStruct(level.shape, level.dtype),
        ],
        compiler_params=pltpu.CompilerParams(vmem_limit_bytes=VMEM_LIMIT),
        cost_estimate=pl.CostEstimate(
            flops=2_000_000_000, bytes_accessed=8_000_000, transcendentals=2_000_000
        ),
        name="cross_attention",
    )(bias, q, k_cross, far1, far2, mean, level)


def final_kernel(weight_ref, sum_ref, peak_ref, total_ref, vc_ref, far_ref, out_ref):
    rows = sum_ref.shape[0]
    n2 = far_ref.shape[1] - 16
    row = grid_of((rows, HD), 0, rows // n2)
    lane = lax.broadcasted_iota(jnp.int32, (rows, HD), 1)
    third = (lane & (n2 - 1)) == row
    pick = jnp.where(third & (lane < 3 * n2), 1.0, 0.0).astype(jnp.bfloat16)
    spread = jnp.where(lane == row, 1.0, 0.0).astype(jnp.bfloat16)[:, :n2]

    def products_of(h):
        cols = slice(h * HD, (h + 1) * HD)
        levels = jnp.concatenate([far_ref[h, n2 : n2 + 16, :]] * (HD // 16), 0)
        return (
            dot_f32(weight_ref[h], with_ones(vc_ref[:, cols])),
            dot_nt(pick, levels),
            dot_f32(spread, far_ref[h, 0:n2, :]),
        )

    following = products_of(0)
    for h in range(STEP_HEADS):
        both, far, far_mean = following
        if h + 1 < STEP_HEADS:
            following = products_of(h + 1)
        cols = slice(h * HD, (h + 1) * HD)
        ahead = far - jnp.broadcast_to(peak_ref[0, :, h : h + 1], (rows, HD))
        near_weight = jnp.exp2(jnp.minimum(-ahead, 0.0))
        far_weight = jnp.exp2(jnp.minimum(ahead, 0.0))
        total = both[:, HD:] + jnp.broadcast_to(total_ref[0, :, h : h + 1], (rows, HD))
        total = near_weight * total + far_weight
        sums = both[:, :HD] + sum_ref[:, cols].astype(jnp.float32)
        sums = near_weight * sums + far_weight * far_mean
        out_ref[:, cols] = (sums * pl.reciprocal(total, approx=True)).astype(jnp.bfloat16)


def final_attention(weights, sums, peak, total, v_cross, far):
    rows, width = sums.shape
    block = pl.BlockSpec((rows, STEP_COLS), lambda i: (0, i))
    levels = pl.BlockSpec((1, rows, HD), lambda i: (i, 0, 0))
    return pl.pallas_call(
        final_kernel,
        grid=(width // STEP_COLS,),
        in_specs=[
            pl.BlockSpec((STEP_HEADS, rows, rows), lambda i: (i, 0, 0)),
            block,
            levels,
            levels,
            block,
            pl.BlockSpec((STEP_HEADS,) + far.shape[1:], lambda i: (i, 0, 0)),
        ],
        out_specs=block,
        out_shape=jax.ShapeDtypeStruct((rows, width), jnp.bfloat16),
        compiler_params=pltpu.CompilerParams(vmem_limit_bytes=VMEM_LIMIT),
        cost_estimate=pl.CostEstimate(
            flops=500_000_000, bytes_accessed=6_000_000, transcendentals=1_000_000
        ),
        name="final_attention",
    )(weights, sums, peak, total, v_cross, far)


def body(queries, keys, values):
    devices = lax.axis_size(AXES)
    inner = lax.axis_size("inner")
    index = lax.axis_index(AXES)
    n2 = queries.shape[0] // 8

    def exchange(value, stride):
        return lax.ppermute(value, AXES, [(i, i ^ stride) for i in range(devices)])

    def cross(value):
        pairs = [(i, i + 1) for i in range(1, devices - 1, 2)]
        return lax.ppermute(value, AXES, pairs + [(j, i) for i, j in pairs])

    k_cross = cross(keys)
    k_mate = exchange(keys, 1)
    v_mate = exchange(values, 1)
    first, heads, last = summaries(queries, keys, values)
    sibling = exchange(last, inner)
    packed = place_sibling(heads, sibling)
    received = lax.all_to_all(packed, "inner", 0, 0, tiled=True)
    far1 = exchange(first, 2)
    v_cross = cross(values)
    far2 = exchange(far1, 1)
    mean, level = chip_attention(queries, keys, values, k_mate, v_mate, far2)
    far = far_attention(received, n2, level)
    far = lax.all_to_all(far, "inner", 0, 0, tiled=True)
    edge = (index == 0) | (index == devices - 1)
    bias = jnp.where(edge, jnp.float32(-1e30), 0.0).reshape(1)
    weights, sums, peak, total = cross_attention(
        bias, queries, k_cross, far1, far2, mean, level
    )
    return final_attention(weights, sums, peak, total, v_cross, far)


def solution(mesh):
    spec = P(AXES, None)
    return jax.shard_map(
        body, mesh=mesh, in_specs=(spec, spec, spec), out_specs=spec, check_vma=False
    )
```

```python
import functools
import math

import jax
import jax.numpy as jnp
from jax import lax
from jax.experimental import pallas as pl
from jax.experimental.pallas import tpu as pltpu
from jax.sharding import PartitionSpec as P

HEADS = 16
HD = 128
AXES = ("outer", "inner")
SCALE = math.log2(math.e) / math.sqrt(HD)
STEP_HEADS = 4
STEP_COLS = STEP_HEADS * HD
VMEM_LIMIT = 60 * 1024 * 1024


def grid_of(shape, axis, span=1):
    return lax.shift_right_logical(
        lax.broadcasted_iota(jnp.int32, shape, axis), jnp.int32(span.bit_length() - 1)
    )


def averaging(rows, cols, row_span, col_span, weight):
    same = grid_of((rows, cols), 0, row_span) == grid_of((rows, cols), 1, col_span)
    return jnp.where(same, weight, 0.0).astype(jnp.bfloat16)


def dot_f32(a, b):
    return lax.dot_general(a, b, (((1,), (0,)), ((), ())), preferred_element_type=jnp.float32)


def dot_nt(a, b):
    return lax.dot_general(a, b, (((1,), (1,)), ((), ())), preferred_element_type=jnp.float32)


def dot_bf16(a, b):
    return dot_f32(a, b).astype(jnp.bfloat16)


def summary_kernel(q_ref, k_ref, v_ref, first_ref, heads_ref, last_ref):
    rows = q_ref.shape[0]
    n1, n2, n4 = rows // 4, rows // 8, rows // 32
    nothing = jnp.zeros((n4, rows), jnp.bfloat16)
    top = [averaging(n1, rows, 1, 4, 1 / 4), averaging(n2, rows, 1, 8, 1 / 8)]
    bottom = averaging(n4, rows, 1, 32, 1 / 32)
    of_k = dot_f32(jnp.concatenate(top + [bottom, nothing], 0), k_ref[...])
    of_v = dot_f32(jnp.concatenate(top + [nothing, bottom], 0), v_ref[...])
    coarse = dot_bf16(top[1], q_ref[...])
    first_ref[0] = of_k[:n1].astype(jnp.bfloat16)
    first_ref[1] = of_v[:n1].astype(jnp.bfloat16)
    second_k = of_k[n1 : n1 + n2].astype(jnp.bfloat16)
    second_v = of_v[n1 : n1 + n2].astype(jnp.bfloat16)
    last = (of_k[n1 + n2 :] + of_v[n1 + n2 :]).astype(jnp.bfloat16)
    for h in range(STEP_HEADS):
        cols = slice(h * HD, (h + 1) * HD)
        heads_ref[h, 0:n2, :] = second_k[:, cols]
        heads_ref[h, n2 : 2 * n2, :] = second_v[:, cols]
        heads_ref[h, 2 * n2 : 3 * n2, :] = coarse[:, cols]
        last_ref[h] = last[:, cols]


def summaries(queries, keys, values):
    rows, width = queries.shape
    block = pl.BlockSpec((rows, STEP_COLS), lambda i: (0, i))
    return pl.pallas_call(
        summary_kernel,
        grid=(width // STEP_COLS,),
        in_specs=[block, block, block],
        out_specs=[
            pl.BlockSpec((2, rows // 4, STEP_COLS), lambda i: (0, 0, i)),
            pl.BlockSpec((STEP_HEADS, 7 * rows // 16, HD), lambda i: (i, 0, 0)),
            pl.BlockSpec((STEP_HEADS, rows // 16, HD), lambda i: (i, 0, 0)),
        ],
        out_shape=[
            jax.ShapeDtypeStruct((2, rows // 4, width), jnp.bfloat16),
            jax.ShapeDtypeStruct((HEADS, 7 * rows // 16, HD), jnp.bfloat16),
            jax.ShapeDtypeStruct((HEADS, rows // 16, HD), jnp.bfloat16),
        ],
        compiler_params=pltpu.CompilerParams(vmem_limit_bytes=VMEM_LIMIT),
        cost_estimate=pl.CostEstimate(flops=400_000_000, bytes_accessed=5_000_000, transcendentals=0),
        name="summaries",
    )(queries, keys, values)


def place_kernel(heads_ref, sibling_ref, out_ref):
    del heads_ref
    out_ref[...] = sibling_ref[...]


def place_sibling(heads, sibling):
    count, rows, _ = sibling.shape
    place = heads.shape[1] // rows - 1
    return pl.pallas_call(
        place_kernel,
        grid=(1,),
        in_specs=[
            pl.BlockSpec(memory_space=pl.ANY),
            pl.BlockSpec((count, rows, HD), lambda i: (0, 0, 0)),
        ],
        out_specs=pl.BlockSpec((count, rows, HD), lambda i: (0, place, 0)),
        out_shape=jax.ShapeDtypeStruct(heads.shape, heads.dtype),
        input_output_aliases={0: 0},
        compiler_params=pltpu.CompilerParams(vmem_limit_bytes=VMEM_LIMIT),
        name="place_sibling",
    )(heads, sibling)


def with_ones(value):
    return jnp.concatenate([value, jnp.ones_like(value)], 1)


def far_kernel(n2, recv_ref, level_ref, out_ref):
    del level_ref
    blocks = recv_ref.shape[0]
    total = blocks * n2
    keys2 = recv_ref[:, 0:n2, :].reshape(total, HD)
    values2 = recv_ref[:, n2 : 2 * n2, :].reshape(total, HD)
    query2 = recv_ref[:, 2 * n2 : 3 * n2, :].reshape(total, HD)
    last = recv_ref[:, 3 * n2 :, :].reshape(-1, HD)
    rows4 = last.shape[0] // 2
    row = lax.broadcasted_iota(jnp.int32, (rows4, 2 * rows4), 0)
    col = lax.broadcasted_iota(jnp.int32, (rows4, 2 * rows4), 1)
    span = n2 // 4
    spot = row + grid_of((rows4, 2 * rows4), 0, span) * span
    keys4 = dot_bf16(jnp.where(col == spot, 1.0, 0.0).astype(jnp.bfloat16), last)
    values4 = dot_bf16(jnp.where(col == spot + span, 1.0, 0.0).astype(jnp.bfloat16), last)
    group = total // 4
    half = averaging(group // 2, group, 1, 2, 0.5)
    keys3 = [dot_bf16(half, keys2[i * group : (i + 1) * group]) for i in range(4)]
    values3 = [dot_bf16(half, values2[i * group : (i + 1) * group]) for i in range(4)]
    spread2 = averaging(group, group, 2, 2, 0.5)
    spread4 = averaging(group, group, 4, 4, 0.25)
    eye = (
        lax.broadcasted_iota(jnp.int32, (group, group), 0)
        == lax.broadcasted_iota(jnp.int32, (group, group), 1)
    )
    group_blocks = blocks // 4
    pad_lane = grid_of((16, group), 1, n2)
    for g in range(4):
        own = query2[g * group : (g + 1) * group]
        sib = g ^ 1
        far = 2 * ((g // 2) ^ 1)
        key3 = jnp.concatenate(keys3[far : far + 2], 0)
        value3 = jnp.concatenate(values3[far : far + 2], 0)
        scores = [
            dot_nt(own, keys2[sib * group : (sib + 1) * group]) * SCALE + 3.0,
            dot_nt(dot_bf16(spread2, own), key3) * SCALE + 4.0,
            dot_nt(dot_bf16(spread4, own), keys4) * SCALE + 5.0,
        ]
        scores = jnp.concatenate(scores, 1)
        peak = jnp.max(scores, axis=1, keepdims=True)
        weights = jnp.exp2(scores - peak).astype(jnp.bfloat16)
        value = jnp.concatenate([values2[sib * group : (sib + 1) * group], value3, values4], 0)
        both = dot_f32(weights, with_ones(value))
        total_weight = both[:, HD:]
        mean = (both[:, :HD] * pl.reciprocal(total_weight, approx=True)).astype(jnp.bfloat16)
        level = peak + jnp.log2(total_weight)
        level_row = jnp.sum(jnp.where(eye, level, 0.0), axis=0, keepdims=True)
        level_rows = jnp.broadcast_to(level_row, (16, group))
        high = level_rows.astype(jnp.bfloat16).astype(jnp.float32)
        rest = level_rows - high
        mid = rest.astype(jnp.bfloat16).astype(jnp.float32)
        low = rest - mid
        for j in range(group_blocks):
            packed = jnp.zeros_like(high)
            for place, part in enumerate((high, mid, low)):
                turned = pltpu.roll(part, (place - j) * n2 % group, 1)
                packed = jnp.where(pad_lane == place, turned, packed)
            out_ref[g * group_blocks + j, 0:n2, :] = mean[j * n2 : (j + 1) * n2]
            out_ref[g * group_blocks + j, n2 : n2 + 16, :] = packed.astype(jnp.bfloat16)


def far_attention(received, n2, level):
    blocks = received.shape[0]
    vmem = pl.BlockSpec(memory_space=pltpu.VMEM)
    return pl.pallas_call(
        functools.partial(far_kernel, n2),
        in_specs=[vmem, pl.BlockSpec(memory_space=pl.ANY)],
        out_specs=vmem,
        out_shape=jax.ShapeDtypeStruct((blocks, n2 + 16, HD), jnp.bfloat16),
        compiler_params=pltpu.CompilerParams(vmem_limit_bytes=48 * 1024 * 1024),
        cost_estimate=pl.CostEstimate(
            flops=200_000_000, bytes_accessed=1_000_000, transcendentals=200_000
        ),
        name="far_attention",
    )(received, level)


def softmax_parts(scores, offsets, top):
    chunks = [[s[:, i : i + HD] for i in range(0, s.shape[1], HD)] for s in scores]
    for parts, offset in zip(chunks, offsets):
        most = functools.reduce(jnp.maximum, parts) * SCALE + offset
        top = most if top is None else jnp.maximum(top, most)
    peak = jnp.broadcast_to(jnp.max(top, axis=1, keepdims=True), top.shape)
    weights = []
    for parts, offset in zip(chunks, offsets):
        shift = peak - offset
        weights += [jnp.exp2(s * SCALE - shift).astype(jnp.bfloat16) for s in parts]
    return weights, peak


def chip_kernel(q_ref, k_ref, v_ref, km_ref, vm_ref, f2_ref, mean_ref, level_ref):
    del f2_ref
    rows = q_ref.shape[0]
    step = pl.program_id(0)
    lane = lax.broadcasted_iota(jnp.int32, (rows, HD), 1)

    def scores_of(h):
        cols = slice(h * HD, (h + 1) * HD)
        return [dot_nt(q_ref[:, cols], ref[:, cols]) for ref in (k_ref, km_ref)]

    levels = jnp.zeros((rows, HD), jnp.float32)
    following = scores_of(0)
    for h in range(STEP_HEADS):
        current = following
        if h + 1 < STEP_HEADS:
            following = scores_of(h + 1)
        cols = slice(h * HD, (h + 1) * HD)
        weights, peak = softmax_parts(current, [0.0, 0.0], None)
        value = jnp.concatenate([v_ref[:, cols], vm_ref[:, cols]], 0)
        both = dot_f32(jnp.concatenate(weights, 1), with_ones(value))
        total = both[:, HD:]
        mean_ref[:, cols] = (both[:, :HD] * pl.reciprocal(total, approx=True)).astype(jnp.bfloat16)
        levels = jnp.where(lane == h, peak + jnp.log2(total), levels)
    level_ref[0] = levels


def chip_attention(q, k, v, k_mate, v_mate, far2):
    rows, width = q.shape
    steps = width // STEP_COLS
    block = pl.BlockSpec((rows, STEP_COLS), lambda i: (0, i))
    return pl.pallas_call(
        chip_kernel,
        grid=(steps,),
        in_specs=[block] * 5 + [pl.BlockSpec(memory_space=pl.ANY)],
        out_specs=[block, pl.BlockSpec((1, rows, HD), lambda i: (i, 0, 0))],
        out_shape=[
            jax.ShapeDtypeStruct((rows, width), jnp.bfloat16),
            jax.ShapeDtypeStruct((steps, rows, HD), jnp.float32),
        ],
        compiler_params=pltpu.CompilerParams(vmem_limit_bytes=VMEM_LIMIT),
        cost_estimate=pl.CostEstimate(
            flops=2_000_000_000, bytes_accessed=7_000_000, transcendentals=2_000_000
        ),
        name="chip_attention",
    )(q, k, v, k_mate, v_mate, far2)


def cross_kernel(
    bias_ref, q_ref, kc_ref, f1_ref, f2_ref, mean_ref, level_ref,
    weight_ref, sum_ref, peak_ref, total_ref,
):
    rows = q_ref.shape[0]
    coarse = dot_bf16(averaging(rows, rows, 4, 4, 0.25), q_ref[...])
    lane = lax.broadcasted_iota(jnp.int32, (rows, HD), 1)
    offsets = [bias_ref[0], 2.0]

    def scores_of(h):
        cols = slice(h * HD, (h + 1) * HD)
        far_key = jnp.concatenate([f1_ref[0, :, cols], f2_ref[0, :, cols]], 0)
        return [dot_nt(q_ref[:, cols], kc_ref[:, cols]), dot_nt(coarse[:, cols], far_key)]

    peaks = jnp.zeros((rows, HD), jnp.float32)
    totals = jnp.zeros((rows, HD), jnp.float32)
    following = scores_of(0)
    for h in range(STEP_HEADS):
        scores = following
        if h + 1 < STEP_HEADS:
            following = scores_of(h + 1)
        cols = slice(h * HD, (h + 1) * HD)
        chip = jnp.broadcast_to(level_ref[0, :, h : h + 1], (rows, HD))
        weights, peak = softmax_parts(scores, offsets, chip)
        weight_ref[h] = jnp.concatenate(weights[:-1], 1)
        value = jnp.concatenate([f1_ref[1, :, cols], f2_ref[1, :, cols]], 0)
        both = dot_f32(weights[-1], with_ones(value))
        chip_weight = jnp.exp2(chip - peak)
        sums = both[:, :HD] + chip_weight * mean_ref[:, cols].astype(jnp.float32)
        sum_ref[:, cols] = sums.astype(jnp.bfloat16)
        peaks = jnp.where(lane == h, peak, peaks)
        totals = jnp.where(lane == h, both[:, HD:] + chip_weight, totals)
    peak_ref[0] = peaks
    total_ref[0] = totals


def cross_attention(bias, q, k_cross, far1, far2, mean, level):
    rows, width = q.shape
    block = pl.BlockSpec((rows, STEP_COLS), lambda i: (0, i))
    far_block = pl.BlockSpec((2, rows // 4, STEP_COLS), lambda i: (0, 0, i))
    levels = pl.BlockSpec((1, rows, HD), lambda i: (i, 0, 0))
    return pl.pallas_call(
        cross_kernel,
        grid=(width // STEP_COLS,),
        in_specs=[pl.BlockSpec(memory_space=pltpu.SMEM)]
        + [block] * 2
        + [far_block] * 2
        + [block, levels],
        out_specs=[pl.BlockSpec((STEP_HEADS, rows, rows), lambda i: (i, 0, 0)), block, levels, levels],
        out_shape=[
            jax.ShapeDtypeStruct((HEADS, rows, rows), jnp.bfloat16),
            jax.ShapeDtypeStruct(mean.shape, mean.dtype),
            jax.ShapeDtypeStruct(level.shape, level.dtype),
            jax.ShapeDtypeStruct(level.shape, level.dtype),
        ],
        compiler_params=pltpu.CompilerParams(vmem_limit_bytes=VMEM_LIMIT),
        cost_estimate=pl.CostEstimate(
            flops=2_000_000_000, bytes_accessed=8_000_000, transcendentals=2_000_000
        ),
        name="cross_attention",
    )(bias, q, k_cross, far1, far2, mean, level)


def gate_kernel(value_ref, other_ref, out_ref):
    del value_ref, other_ref, out_ref


def gate(value, other):
    anywhere = pl.BlockSpec(memory_space=pl.ANY)
    return pl.pallas_call(
        gate_kernel,
        in_specs=[anywhere, anywhere],
        out_specs=anywhere,
        out_shape=jax.ShapeDtypeStruct(value.shape, value.dtype),
        input_output_aliases={0: 0},
        compiler_params=pltpu.CompilerParams(vmem_limit_bytes=VMEM_LIMIT),
        cost_estimate=pl.CostEstimate(
            flops=500_000_000, bytes_accessed=6_000_000, transcendentals=100_000
        ),
        name="gate",
    )(value, other)


def final_kernel(weight_ref, sum_ref, peak_ref, total_ref, vc_ref, far_ref, out_ref):
    rows = sum_ref.shape[0]
    n2 = far_ref.shape[1] - 16
    row = grid_of((rows, HD), 0, rows // n2)
    lane = lax.broadcasted_iota(jnp.int32, (rows, HD), 1)
    third = (lane & (n2 - 1)) == row
    pick = jnp.where(third & (lane < 3 * n2), 1.0, 0.0).astype(jnp.bfloat16)
    spread = jnp.where(lane == row, 1.0, 0.0).astype(jnp.bfloat16)[:, :n2]

    def products_of(h):
        cols = slice(h * HD, (h + 1) * HD)
        levels = jnp.concatenate([far_ref[h, n2 : n2 + 16, :]] * (HD // 16), 0)
        return (
            dot_f32(weight_ref[h], with_ones(vc_ref[:, cols])),
            dot_nt(pick, levels),
            dot_f32(spread, far_ref[h, 0:n2, :]),
        )

    following = products_of(0)
    for h in range(STEP_HEADS):
        both, far, far_mean = following
        if h + 1 < STEP_HEADS:
            following = products_of(h + 1)
        cols = slice(h * HD, (h + 1) * HD)
        ahead = far - jnp.broadcast_to(peak_ref[0, :, h : h + 1], (rows, HD))
        near_weight = jnp.exp2(jnp.minimum(-ahead, 0.0))
        far_weight = jnp.exp2(jnp.minimum(ahead, 0.0))
        total = both[:, HD:] + jnp.broadcast_to(total_ref[0, :, h : h + 1], (rows, HD))
        total = near_weight * total + far_weight
        sums = both[:, :HD] + sum_ref[:, cols].astype(jnp.float32)
        sums = near_weight * sums + far_weight * far_mean
        out_ref[:, cols] = (sums * pl.reciprocal(total, approx=True)).astype(jnp.bfloat16)


def final_attention(weights, sums, peak, total, v_cross, far):
    rows, width = sums.shape
    block = pl.BlockSpec((rows, STEP_COLS), lambda i: (0, i))
    levels = pl.BlockSpec((1, rows, HD), lambda i: (i, 0, 0))
    return pl.pallas_call(
        final_kernel,
        grid=(width // STEP_COLS,),
        in_specs=[
            pl.BlockSpec((STEP_HEADS, rows, rows), lambda i: (i, 0, 0)),
            block,
            levels,
            levels,
            block,
            pl.BlockSpec((STEP_HEADS,) + far.shape[1:], lambda i: (i, 0, 0)),
        ],
        out_specs=block,
        out_shape=jax.ShapeDtypeStruct((rows, width), jnp.bfloat16),
        compiler_params=pltpu.CompilerParams(vmem_limit_bytes=56 * 1024 * 1024),
        cost_estimate=pl.CostEstimate(
            flops=500_000_000, bytes_accessed=6_000_000, transcendentals=1_000_000
        ),
        name="final_attention",
    )(weights, sums, peak, total, v_cross, far)


def body(queries, keys, values):
    devices = lax.axis_size(AXES)
    inner = lax.axis_size("inner")
    index = lax.axis_index(AXES)
    n2 = queries.shape[0] // 8

    def exchange(value, stride):
        return lax.ppermute(value, AXES, [(i, i ^ stride) for i in range(devices)])

    def cross(value):
        pairs = [(i, i + 1) for i in range(1, devices - 1, 2)]
        return lax.ppermute(value, AXES, pairs + [(j, i) for i, j in pairs])

    k_cross = cross(keys)
    k_mate = exchange(keys, 1)
    v_mate = exchange(values, 1)
    first, heads, last = summaries(queries, keys, values)
    sibling = exchange(last, inner)
    packed = place_sibling(heads, sibling)
    received = lax.all_to_all(packed, "inner", 0, 0, tiled=True)
    far1 = exchange(first, 2)
    v_cross = cross(values)
    far2 = exchange(far1, 1)
    mean, level = chip_attention(queries, keys, values, k_mate, v_mate, far2)
    far = far_attention(received, n2, level)
    far = lax.all_to_all(far, "inner", 0, 0, tiled=True)
    edge = (index == 0) | (index == devices - 1)
    bias = jnp.where(edge, jnp.float32(-1e30), 0.0).reshape(1)
    weights, sums, peak, total = cross_attention(
        bias, queries, k_cross, far1, far2, mean, level
    )
    v_cross = gate(v_cross, peak)
    return final_attention(weights, sums, peak, total, v_cross, far)


def solution(mesh):
    spec = P(AXES, None)
    return jax.shard_map(
        body, mesh=mesh, in_specs=(spec, spec, spec), out_specs=spec, check_vma=False
    )
```
